32 devices in a mesh: groups: 2 (over y), ex: 4 (over z), layer: 2 (over x), rep: 2 (over core).
Axes of the slice: x: 2, y: 2, z: 4, core: 2. Of those that a mesh axis runs over, the one named last changes fastest.
Arguments:
- features: bfloat16 [8192, 4, 256], P(('groups', 'ex'), 'layer'), parts along dimension 0, may hold values from -6 to 6
- pair_list: int32 [3, 8, 4], P(None, ('groups', 'ex'), 'rep'), parts along dimension 1, may hold values from 0 to 3, as said below
- pair_count: int32 [8, 2], P(('groups', 'ex'), 'rep'), parts along dimension 0, may hold values from 1 to 2
Outputs:
- scores: float32 [8192], P(('groups', 'ex')), parts along dimension 0
The draws below stay inside these ranges and needn't reach their ends.
There are 2 independent parts, one for each index of `groups`. The reference program is written for one: setup_inputs(seed, part) draws one part's arguments, and reference() takes and returns one part's arrays. A program takes and returns all parts, laid end to end along the dimension named above; each array names one. Nothing has to cross between parts.
Inputs may be any that keep to these rules, and one draw needn't show every extreme that they name: `pair_list`: row 0 names a block of the owner itself and row 2 a block of the owner named in row 1, both in 0 to 3; row 1 is in 0 to 3, and the 4 entries of row 1 of one owner are all different. Only the first pair_count entries of each index of rep are read.
All inputs are finite; a program needn't handle non-finite values.
Results may differ from the reference program's by a relative error of at most 0.004.
Values may be sent and summed in bfloat16 or wider, within the bound.
A program may use at most 64 MiB of HBM per device.

```python
import jax
import jax.numpy as jnp
from jax import lax

BLK = 256
FEAT = 256
MOD_DEV = 2
BLK_DEV = 4
SLOTS = 2
MODULES = 4
EXAMPLES = 4096
N_EX = 4
N_LAYER = 2
N_REP = 2


def draw_pair_list(key, part):
    key = jax.random.fold_in(key, 11)
    keys = jax.random.split(key, N_EX + 3)
    owners = jax.vmap(lambda single: jax.random.permutation(single, N_EX))(keys[:N_EX]).astype(jnp.int32)
    chosen = jax.random.randint(keys[N_EX + 2], (), 0, N_EX)
    is_chosen = (jnp.arange(N_EX, dtype=jnp.int32) == chosen)[:, None]
    first = owners[:, 0:1]
    last_owner = jnp.int32(N_EX - 1)
    swapped = jnp.where(owners == first, last_owner, jnp.where(owners == last_owner, first, owners))
    owners = jnp.where(is_chosen, swapped, owners)
    owners = owners[:, :N_REP * SLOTS].astype(jnp.int32)
    mine = jax.random.randint(keys[N_EX], (N_EX, N_REP * SLOTS), 0, BLK_DEV).astype(jnp.int32)
    other = jax.random.randint(keys[N_EX + 1], (N_EX, N_REP * SLOTS), 0, BLK_DEV).astype(jnp.int32)
    first_slot = (jnp.arange(N_REP * SLOTS, dtype=jnp.int32) == 0)[None, :] & is_chosen
    mine = jnp.where(first_slot, jnp.int32(BLK_DEV - 1), mine)
    other = jnp.where(first_slot, jnp.int32(0), other)
    return jnp.stack([mine, owners, other]).astype(jnp.int32)


def draw_pair_count(key, part):
    key = jax.random.fold_in(key, 23)
    first_key, second_key, third_key = jax.random.split(key, 3)
    lowest = max(1, SLOTS // 2)
    drawn = jax.random.randint(first_key, (N_EX * N_REP,), lowest, SLOTS + 1)
    busiest = jax.random.randint(second_key, (), 0, N_EX * N_REP)
    offset = jax.random.randint(third_key, (), 1, N_EX * N_REP)
    lightest = (busiest + offset) % (N_EX * N_REP)
    positions = jnp.arange(N_EX * N_REP)
    filled = jnp.where(positions == busiest, SLOTS, jnp.where(positions == lightest, lowest, drawn))
    return filled.reshape(N_EX, N_REP).astype(jnp.int32)


def steps_of(rng, dims, shards, smallest, top_value):
    loudness, own = 1.0, jax.random.fold_in(rng, 6)
    for position, shards_of in shards:
        steps = jnp.exp(jax.random.uniform(jax.random.fold_in(own, position), (shards_of,), jnp.float32, smallest / len(shards), top_value / len(shards)))
        loudness = loudness * jnp.repeat(steps, dims[position] // shards_of).reshape([-1 if axis == position else 1 for axis in range(len(dims))])
    return loudness


def gaussian(own_key, extent, spread, most, pieces=(), kind=jnp.bfloat16):
    gain = steps_of(own_key, extent, pieces, -0.22, 0.18) if pieces else 1.0
    values = jax.random.normal(own_key, extent, jnp.float32) * spread * gain
    return jnp.minimum(jnp.maximum(values, -most), most).astype(kind)


def setup_inputs(seed: int = 0, part: int = 0) -> dict:
    streams_of = jax.random.split(jax.random.key(seed), 4)
    part_keys = jax.random.split(jax.random.fold_in(streams_of[3], part), 4)
    features = gaussian(part_keys[0], (EXAMPLES, MODULES, FEAT), 1.0, 6.0, ((0, 4), (1, 2)))
    pair_list = draw_pair_list(jax.random.fold_in(jax.random.fold_in(streams_of[3], part), 71), part)
    pair_count = draw_pair_count(jax.random.fold_in(jax.random.fold_in(streams_of[3], part), 71), part)
    return {"features": features, "pair_list": pair_list, "pair_count": pair_count}


def reference(features, pair_list, pair_count):
    flat = features.reshape(EXAMPLES, MODULES * FEAT)
    squares = lax.optimization_barrier(jnp.sum(jnp.square(flat.astype(jnp.float32)), axis=1))
    unit = (flat.astype(jnp.float32) * lax.rsqrt(squares + 1e-06)[:, None]).astype(jnp.bfloat16)
    grouped = unit.reshape(N_EX * BLK_DEV, BLK, N_LAYER, MOD_DEV * FEAT)
    owner_ids = jnp.broadcast_to(jnp.arange(N_EX, dtype=jnp.int32)[:, None], (N_EX, N_REP * SLOTS))
    slot_ids = jnp.broadcast_to(jnp.arange(N_REP * SLOTS, dtype=jnp.int32)[None, :], (N_EX, N_REP * SLOTS))
    half_ids = slot_ids // SLOTS
    alive = (slot_ids % SLOTS < pair_count[owner_ids, half_ids]).reshape(-1)
    row_block = (owner_ids * BLK_DEV + pair_list[0]).reshape(-1).astype(jnp.int32)
    column_block = (pair_list[1] * BLK_DEV + pair_list[2]).reshape(-1).astype(jnp.int32)
    diagonal = jnp.arange(BLK)[:, None] == jnp.arange(BLK)[None, :]

    def one_pair(entry):
        row_index, column_index, living = entry
        left = grouped[row_index].astype(jnp.float32)
        right = grouped[column_index].astype(jnp.float32)
        partial_value = jnp.einsum('igf,jgf->gij', left, right).astype(jnp.bfloat16)
        partial_value = lax.optimization_barrier(partial_value)
        dots = lax.optimization_barrier(jnp.sum(partial_value.astype(jnp.float32), axis=0))
        keep = living & jnp.logical_not((row_index == column_index) & diagonal)
        kernel = jnp.where(keep, jnp.exp(20.0 * dots), jnp.zeros_like(dots))
        return (lax.optimization_barrier(jnp.sum(kernel, axis=1)), lax.optimization_barrier(jnp.sum(kernel, axis=0)))
    row_sums, column_sums = lax.map(one_pair, (row_block, column_block, alive))
    totals = jnp.zeros((N_EX * BLK_DEV, BLK), jnp.float32)
    totals = totals.at[row_block].add(row_sums).at[column_block].add(column_sums)
    return jnp.log1p(totals.reshape(-1) / BLK)
```

```python
import functools

import jax
import jax.numpy as jnp
from jax import lax
from jax.experimental import pallas as pl
from jax.experimental.pallas import tpu as pltpu
from jax.sharding import PartitionSpec as P

BLK = 256
MESH = pl.DeviceIdType.MESH
CONTRACT_LAST = (((1,), (1,)), ((), ()))


def body(N, L, R, feat, plist, pcount, out, tab, stage, arow, csend, crecv, sq, isend, irecv, xsend, xrecv,
         rsend, rrecv, ctab, tab_s, tab_r, a_s, a_r, c_s, c_r, q_s, q_r, i_s, i_r, x_s, x_r, r_s, r_r, t_s, t_r):
    NB = feat.shape[0]
    slots = plist.shape[2]
    J = N // R
    HB = BLK // L
    e, l, r = lax.axis_index("ex"), lax.axis_index("layer"), lax.axis_index("rep")

    def place(d, dl, dr):
        return {"ex": lax.rem(e + d, N), "layer": lax.rem(l + dl, L), "rep": lax.rem(r + dr, R)}

    def remote(src, dst, ss, rs, target):
        return pltpu.make_async_remote_copy(
            src_ref=src, dst_ref=dst, send_sem=ss, recv_sem=rs, device_id=target, device_id_type=MESH
        )

    barrier = pltpu.get_barrier_semaphore()

    def greet(i, carry):
        pl.semaphore_signal(
            barrier, inc=1, device_id=place(i // (L * R), lax.rem(i // R, L), lax.rem(i, R)), device_id_type=MESH
        )
        return carry

    lax.fori_loop(1, N * L * R, greet, 0)

    rows_iota = lax.broadcasted_iota(jnp.int32, tab.shape[1:], 0)
    table = jnp.zeros(tab.shape[1:], jnp.int32)
    count = pcount[0, 0]
    for s in range(slots):
        code = jnp.where(s < count, 1 + plist[0, 0, s] + 256 * plist[2, 0, s], 0)
        table = table + jnp.where(rows_iota == plist[1, 0, s], code, 0)
    tab[r] = table

    pl.semaphore_wait(barrier, N * L * R - 1)

    tab_copies = []
    for dr in range(1, R):
        copy = remote(tab.at[r], tab.at[r], tab_s.at[dr - 1], tab_r.at[dr - 1], place(0, 0, dr))
        copy.start()
        tab_copies.append(copy)

    ones = jnp.ones((8, feat.shape[2]), jnp.bfloat16)
    for b in range(NB):
        x = feat[b].astype(jnp.float32)
        x2 = x * x
        high = x2.astype(jnp.bfloat16)
        low = (x2 - high.astype(jnp.float32)).astype(jnp.bfloat16)
        s2 = lax.dot_general(ones, high, CONTRACT_LAST, preferred_element_type=jnp.float32)
        s2 = s2 + lax.dot_general(ones, low, CONTRACT_LAST, preferred_element_type=jnp.float32)
        sq[l, b : b + 1, :] = s2[0:1, :]

    q_copies = []
    for dl in range(1, L):
        copy = remote(sq.at[l], sq.at[l], q_s.at[dl - 1], q_r.at[dl - 1], place(0, dl, 0))
        copy.start()
        q_copies.append(copy)

    for copy in tab_copies:
        copy.wait()
    table = tab[0]
    for i in range(1, R):
        table = table + tab[i]

    codes, a_copies, c_copies = [], [], []
    for j in range(J):
        d = R * j + r
        p = lax.rem(e + d, N)
        code = jnp.max(jnp.where(rows_iota == p, table, 0))
        codes.append(code)
        mine = jnp.maximum(code - 1, 0) & 255
        stage[j] = feat[mine]
        csend[j] = jnp.full(csend.shape[1:], code, jnp.int32)
        target = {"ex": p}
        a_copy = remote(stage.at[j], arow.at[j], a_s.at[j], a_r.at[j], target)
        c_copy = remote(csend.at[j], crecv.at[j], c_s.at[j], c_r.at[j], target)
        if j == 0:

            @pl.when(r == 0)
            def _():
                arow[0] = stage[0]
                crecv[0] = csend[0]

            @pl.when(r != 0)
            def _():
                a_copy.start()
                c_copy.start()

        else:
            a_copy.start()
            c_copy.start()
        a_copies.append(a_copy)
        c_copies.append(c_copy)

    for copy in q_copies:
        copy.wait()
    total_sq = sq[0]
    for i in range(1, L):
        total_sq = total_sq + sq[i]
    inv = lax.rsqrt(total_sq + 1e-06)

    i_copies = []
    for j in range(J):
        mine = jnp.maximum(codes[j] - 1, 0) & 255
        pick = jnp.zeros((1, BLK), jnp.float32)
        for b in range(NB):
            pick = jnp.where(mine == b, inv[b : b + 1, :], pick)
        isend[j] = pick
        copy = remote(isend.at[j], irecv.at[j], i_s.at[j], i_r.at[j], {"ex": lax.rem(e + R * j + r, N)})
        if j == 0:

            @pl.when(r == 0)
            def _():
                irecv[0] = isend[0]

            @pl.when(r != 0)
            def _():
                copy.start()

        else:
            copy.start()
        i_copies.append(copy)

    at_row = lax.broadcasted_iota(jnp.int32, (HB, BLK), 0) + l * HB
    at_column = lax.broadcasted_iota(jnp.int32, (HB, BLK), 1)
    spot = at_row == at_column
    columns = [jnp.zeros((1, BLK), jnp.float32) for _ in range(NB)]
    x_copies, own, rights = [], [], []
    for j in range(J):
        if j == 0:

            @pl.when(r != 0)
            def _():
                c_copies[0].wait()
                a_copies[0].wait()
                i_copies[0].wait()

        else:
            c_copies[j].wait()
            a_copies[j].wait()
            i_copies[j].wait()
        code = jnp.max(crecv[j])
        peer = jnp.maximum(code - 1, 0) // 256
        right = feat[peer]
        rights.append((code, peer))
        for dl in range(1, L):
            other = lax.rem(l + dl, L)
            left = arow[j, pl.ds(pl.multiple_of(other * HB, HB), HB), :]
            part = lax.dot_general(left, right, CONTRACT_LAST, preferred_element_type=jnp.float32)
            xsend[j, dl - 1] = part.astype(jnp.bfloat16)
            copy = remote(
                xsend.at[j, dl - 1], xrecv.at[j, dl - 1], x_s.at[j, dl - 1], x_r.at[j, dl - 1], place(0, dl, 0)
            )
            copy.start()
            x_copies.append(copy)
        left = arow[j, pl.ds(pl.multiple_of(l * HB, HB), HB), :]
        own.append(lax.dot_general(left, right, CONTRACT_LAST, preferred_element_type=jnp.float32))

    r_copies = []
    for j in range(J):
        dots = own[j]
        for dl in range(1, L):
            x_copies[j * (L - 1) + dl - 1].wait()
            dots = dots + xrecv[j, dl - 1].astype(jnp.float32)
        code, peer = rights[j]
        inv_row = jnp.sum(jnp.where(spot, irecv[j], 0.0), axis=1, keepdims=True)
        inv_column = jnp.zeros((1, BLK), jnp.float32)
        for b in range(NB):
            inv_column = jnp.where(peer == b, inv[b : b + 1, :], inv_column)
        kern = jnp.exp(20.0 * (dots * inv_row * inv_column))
        if j == 0:
            same = (r == 0) & ((jnp.maximum(code - 1, 0) & 255) == peer)
            kern = jnp.where(spot, kern * jnp.where(same, 0.0, 1.0), kern)
        row_sums = jnp.sum(kern, axis=1, keepdims=True)
        rsend[j] = jnp.sum(jnp.where(spot, row_sums, 0.0), axis=0, keepdims=True)
        column_sums = jnp.sum(kern, axis=0, keepdims=True)
        for b in range(NB):
            columns[b] = columns[b] + jnp.where((peer == b) & (code > 0), column_sums, 0.0)
        slot = e * L + l
        back = N - (R * j + r)
        for dl in range(L):
            for dr in range(R):
                k = dl * R + dr
                copy = remote(rsend.at[j], rrecv.at[slot], r_s.at[j, k], r_r.at[slot], place(back, dl, dr))
                if j == 0 and k == 0:

                    @pl.when(r == 0)
                    def _():
                        rrecv[slot] = rsend[0]

                    @pl.when(r != 0)
                    def _():
                        copy.start()

                else:
                    copy.start()
                r_copies.append(copy)

    mine_slot = l * R + r
    for b in range(NB):
        ctab[mine_slot, b : b + 1, :] = columns[b]
    t_copies = []
    for k in range(1, L * R):
        copy = remote(
            ctab.at[mine_slot], ctab.at[mine_slot], t_s.at[k - 1], t_r.at[k - 1], place(0, k // R, k % R)
        )
        copy.start()
        t_copies.append(copy)

    for k in range(1, L * R):
        t_copies[k - 1].wait()
    for d in range(N):
        p = lax.rem(e + d, N)
        for dl in range(L):
            slot = p * L + lax.rem(l + dl, L)
            copy = remote(rsend.at[0], rrecv.at[slot], r_s.at[0, 0], r_r.at[slot], place(0, 0, 1))
            if d == 0 and dl == 0:

                @pl.when(r != 0)
                def _():
                    copy.wait_recv()

            else:
                copy.wait_recv()

    totals = ctab[0]
    for i in range(1, L * R):
        totals = totals + ctab[i]
    block_iota = lax.broadcasted_iota(jnp.int32, (NB, BLK), 0)
    for p in range(N):
        got = rrecv[p * L]
        for i in range(1, L):
            got = got + rrecv[p * L + i]
        code = table[p : p + 1, :]
        code = jnp.concatenate([code] * (BLK // 128), axis=1)
        live = (code > 0) & ((jnp.maximum(code - 1, 0) & 255) == block_iota)
        totals = totals + jnp.where(live, got, 0.0)
    for b in range(NB):
        for h in range(BLK // 128):
            out[b * (BLK // 128) + h : b * (BLK // 128) + h + 1, :] = totals[b : b + 1, h * 128 : (h + 1) * 128]

    for n, copy in enumerate(r_copies):
        if n == 0:

            @pl.when(r != 0)
            def _():
                r_copies[0].wait_send()

        else:
            copy.wait_send()


def on_device(sizes, features, pair_list, pair_count):
    N, L, R = sizes
    rows = features.shape[0]
    blocks = features.reshape(rows // BLK, BLK, -1)
    NB, _, width = blocks.shape
    J = N // R
    HB = BLK // L
    table_rows = -(-N // 8) * 8
    dma = pltpu.SemaphoreType.DMA
    vmem = pl.BlockSpec(memory_space=pltpu.VMEM)
    smem = pl.BlockSpec(memory_space=pltpu.SMEM)
    totals = pl.pallas_call(
        functools.partial(body, N, L, R),
        out_shape=jax.ShapeDtypeStruct((rows // 128, 128), jnp.float32),
        in_specs=[vmem, smem, smem],
        out_specs=vmem,
        scratch_shapes=[
            pltpu.VMEM((R, table_rows, 128), jnp.int32),
            pltpu.VMEM((J, BLK, width), jnp.bfloat16),
            pltpu.VMEM((J, BLK, width), jnp.bfloat16),
            pltpu.VMEM((J, 8, 128), jnp.int32),
            pltpu.VMEM((J, 8, 128), jnp.int32),
            pltpu.VMEM((L, NB, BLK), jnp.float32),
            pltpu.VMEM((J, 1, BLK), jnp.float32),
            pltpu.VMEM((J, 1, BLK), jnp.float32),
            pltpu.VMEM((J, L - 1, HB, BLK), jnp.bfloat16),
            pltpu.VMEM((J, L - 1, HB, BLK), jnp.bfloat16),
            pltpu.VMEM((J, 1, BLK), jnp.float32),
            pltpu.VMEM((N * L, 1, BLK), jnp.float32),
            pltpu.VMEM((L * R, NB, BLK), jnp.float32),
            dma((R - 1,)), dma((R - 1,)),
            dma((J,)), dma((J,)),
            dma((J,)), dma((J,)),
            dma((L - 1,)), dma((L - 1,)),
            dma((J,)), dma((J,)),
            dma((J, L - 1)), dma((J, L - 1)),
            dma((J, L * R)), dma((N * L,)),
            dma((L * R - 1,)), dma((L * R - 1,)),
        ],
        compiler_params=pltpu.CompilerParams(
            collective_id=0, has_side_effects=True, vmem_limit_bytes=48 * 1024 * 1024
        ),
    )(blocks, pair_list, pair_count)
    return jnp.log1p(totals / BLK).reshape(-1)


def solution(mesh):
    sizes = (mesh.shape["ex"], mesh.shape["layer"], mesh.shape["rep"])
    return jax.shard_map(
        functools.partial(on_device, sizes),
        mesh=mesh,
        in_specs=(
            P(("groups", "ex"), "layer", None),
            P(None, ("groups", "ex"), "rep"),
            P(("groups", "ex"), "rep"),
        ),
        out_specs=P(("groups", "ex")),
        check_vma=False,
    )
```

```python
import functools

import jax
import jax.numpy as jnp
from jax import lax
from jax.experimental import pallas as pl
from jax.experimental.pallas import tpu as pltpu
from jax.sharding import PartitionSpec as P

BLK = 256
MESH = pl.DeviceIdType.MESH
CONTRACT_LAST = (((1,), (1,)), ((), ()))


def body(N, L, R, feat, plist, pcount, out, tab, stage, arow, csend, crecv, sq, isend, irecv, xsend, xrecv,
         rsend, rrecv, ctab, tab_s, tab_r, a_s, a_r, c_s, c_r, q_s, q_r, i_s, i_r, x_s, x_r, r_s, r_r, t_s, t_r):
    NB = feat.shape[0]
    slots = plist.shape[1]
    J = N // R
    HB = BLK // L
    e, l, r = lax.axis_index("ex"), lax.axis_index("layer"), lax.axis_index("rep")

    def place(d, dl, dr):
        return {"ex": lax.rem(e + d, N), "layer": lax.rem(l + dl, L), "rep": lax.rem(r + dr, R)}

    def remote(src, dst, ss, rs, target):
        return pltpu.make_async_remote_copy(
            src_ref=src, dst_ref=dst, send_sem=ss, recv_sem=rs, device_id=target, device_id_type=MESH
        )

    barrier = pltpu.get_barrier_semaphore()

    def greet(i, carry):
        pl.semaphore_signal(
            barrier, inc=1, device_id=place(i // (L * R), lax.rem(i // R, L), lax.rem(i, R)), device_id_type=MESH
        )
        return carry

    lax.fori_loop(1, N * L * R, greet, 0)

    rows_iota = lax.broadcasted_iota(jnp.int32, tab.shape[1:], 0)
    table = jnp.zeros(tab.shape[1:], jnp.int32)
    count = pcount[0, 0]
    for s in range(slots):
        code = jnp.where(s < count, 1 + plist[0, s, 0] + 256 * plist[0, s, 2], 0)
        table = table + jnp.where(rows_iota == plist[0, s, 1], code, 0)
    tab[r] = table

    ones = jnp.ones((8, feat.shape[2]), jnp.bfloat16)
    for b in range(NB):
        x = feat[b].astype(jnp.float32)
        x2 = x * x
        high = x2.astype(jnp.bfloat16)
        low = (x2 - high.astype(jnp.float32)).astype(jnp.bfloat16)
        s2 = lax.dot_general(ones, high, CONTRACT_LAST, preferred_element_type=jnp.float32)
        s2 = s2 + lax.dot_general(ones, low, CONTRACT_LAST, preferred_element_type=jnp.float32)
        sq[l, b : b + 1, :] = s2[0:1, :]

    pl.semaphore_wait(barrier, N * L * R - 1)

    tab_copies = []
    for dr in range(1, R):
        copy = remote(tab.at[r], tab.at[r], tab_s.at[dr - 1], tab_r.at[dr - 1], place(0, 0, dr))
        copy.start()
        tab_copies.append(copy)

    q_copies = []
    for dl in range(1, L):
        copy = remote(sq.at[l], sq.at[l], q_s.at[dl - 1], q_r.at[dl - 1], place(0, dl, 0))
        copy.start()
        q_copies.append(copy)

    for copy in tab_copies:
        copy.wait()
    table = tab[0]
    for i in range(1, R):
        table = table + tab[i]

    def part_rows(dl):
        return pl.ds(pl.multiple_of(lax.rem(l + dl, L) * HB, HB), HB)

    order = list(range(1, L)) + [0]
    codes, c_copies = [], []
    a_copies = {}
    for j in range(J):
        p = lax.rem(e + R * j + r, N)
        code = jnp.max(jnp.where(rows_iota == p, table, 0))
        codes.append(code)
        mine = jnp.maximum(code - 1, 0) & 255
        stage[j] = feat[mine]
        csend[j] = jnp.full(csend.shape[1:], code, jnp.int32)
        target = {"ex": p}
        c_copy = remote(csend.at[j], crecv.at[j], c_s.at[j], c_r.at[j], target)
        c_copies.append(c_copy)
        for dl in order:
            a_copies[j, dl] = remote(
                stage.at[j, part_rows(dl)], arow.at[j, part_rows(dl)], a_s.at[j, dl], a_r.at[j, dl], target
            )
        if j == 0:

            @pl.when(r == 0)
            def _():
                arow[0] = stage[0]
                crecv[0] = csend[0]

            @pl.when(r != 0)
            def _():
                c_copy.start()
                for dl in order[:-1]:
                    a_copies[0, dl].start()

        else:
            c_copy.start()
            for dl in order[:-1]:
                a_copies[j, dl].start()
    for j in range(J):
        if j == 0:

            @pl.when(r != 0)
            def _():
                a_copies[0, 0].start()

        else:
            a_copies[j, 0].start()

    for copy in q_copies:
        copy.wait()
    total_sq = sq[0]
    for i in range(1, L):
        total_sq = total_sq + sq[i]
    inv = lax.rsqrt(total_sq + 1e-06)

    i_copies = []
    for j in range(J):
        mine = jnp.maximum(codes[j] - 1, 0) & 255
        pick = jnp.zeros((1, BLK), jnp.float32)
        for b in range(NB):
            pick = jnp.where(mine == b, inv[b : b + 1, :], pick)
        isend[j] = pick
        copy = remote(isend.at[j], irecv.at[j], i_s.at[j], i_r.at[j], {"ex": lax.rem(e + R * j + r, N)})
        if j == 0:

            @pl.when(r == 0)
            def _():
                irecv[0] = isend[0]

            @pl.when(r != 0)
            def _():
                copy.start()

        else:
            copy.start()
        i_copies.append(copy)

    at_row = lax.broadcasted_iota(jnp.int32, (HB, BLK), 0) + l * HB
    at_column = lax.broadcasted_iota(jnp.int32, (HB, BLK), 1)
    spot = at_row == at_column
    columns = [jnp.zeros((1, BLK), jnp.float32) for _ in range(NB)]
    x_copies, rights = {}, []

    def arrived(j, *copies):
        if j == 0:

            @pl.when(r != 0)
            def _():
                for copy in copies:
                    copy.wait_recv()

        else:
            for copy in copies:
                copy.wait_recv()

    for j in range(J):
        arrived(j, c_copies[j])
        code = jnp.max(crecv[j])
        peer = jnp.maximum(code - 1, 0) // 256
        rights.append((code, peer))
        for dl in range(1, L):
            arrived(j, a_copies[j, dl])
            part = lax.dot_general(
                arow[j, part_rows(dl), :], feat[peer], CONTRACT_LAST, preferred_element_type=jnp.float32
            )
            xsend[j, dl - 1] = part.astype(jnp.bfloat16)
            copy = remote(
                xsend.at[j, dl - 1], xrecv.at[j, dl - 1], x_s.at[j, dl - 1], x_r.at[j, dl - 1], place(0, dl, 0)
            )
            copy.start()
            x_copies[j, dl] = copy

    r_copies = []
    for j in range(J):
        arrived(j, a_copies[j, 0], i_copies[j])
        dots = lax.dot_general(
            arow[j, part_rows(0), :], feat[rights[j][1]], CONTRACT_LAST, preferred_element_type=jnp.float32
        )
        for dl in range(1, L):
            x_copies[j, dl].wait_recv()
            dots = dots + xrecv[j, dl - 1].astype(jnp.float32)
        code, peer = rights[j]
        inv_row = jnp.sum(jnp.where(spot, irecv[j], 0.0), axis=1, keepdims=True)
        inv_column = jnp.zeros((1, BLK), jnp.float32)
        for b in range(NB):
            inv_column = jnp.where(peer == b, inv[b : b + 1, :], inv_column)
        kern = jnp.exp(20.0 * (dots * inv_row * inv_column))
        if j == 0:
            same = (r == 0) & ((jnp.maximum(code - 1, 0) & 255) == peer)
            kern = jnp.where(spot, kern * jnp.where(same, 0.0, 1.0), kern)
        row_sums = jnp.sum(kern, axis=1, keepdims=True)
        rsend[j] = jnp.sum(jnp.where(spot, row_sums, 0.0), axis=0, keepdims=True)
        column_sums = jnp.sum(kern, axis=0, keepdims=True)
        for b in range(NB):
            columns[b] = columns[b] + jnp.where((peer == b) & (code > 0), column_sums, 0.0)
        slot = e * L + l
        back = N - (R * j + r)
        for dl in range(L):
            for dr in range(R):
                k = dl * R + dr
                copy = remote(rsend.at[j], rrecv.at[slot], r_s.at[j, k], r_r.at[slot], place(back, dl, dr))
                if j == 0 and k == 0:

                    @pl.when(r == 0)
                    def _():
                        rrecv[slot] = rsend[0]

                    @pl.when(r != 0)
                    def _():
                        copy.start()

                else:
                    copy.start()
                r_copies.append(copy)

    mine_slot = l * R + r
    for b in range(NB):
        ctab[mine_slot, b : b + 1, :] = columns[b]
    t_copies = []
    for k in range(1, L * R):
        copy = remote(
            ctab.at[mine_slot], ctab.at[mine_slot], t_s.at[k - 1], t_r.at[k - 1], place(0, k // R, k % R)
        )
        copy.start()
        t_copies.append(copy)

    for k in range(1, L * R):
        t_copies[k - 1].wait()
    for d in range(N):
        p = lax.rem(e + d, N)
        for dl in range(L):
            slot = p * L + lax.rem(l + dl, L)
            copy = remote(rsend.at[0], rrecv.at[slot], r_s.at[0, 0], r_r.at[slot], place(0, 0, 1))
            if d == 0 and dl == 0:

                @pl.when(r != 0)
                def _():
                    copy.wait_recv()

            else:
                copy.wait_recv()

    totals = ctab[0]
    for i in range(1, L * R):
        totals = totals + ctab[i]
    block_iota = lax.broadcasted_iota(jnp.int32, (NB, BLK), 0)
    for p in range(N):
        got = rrecv[p * L]
        for i in range(1, L):
            got = got + rrecv[p * L + i]
        code = table[p : p + 1, :]
        code = jnp.concatenate([code] * (BLK // 128), axis=1)
        live = (code > 0) & ((jnp.maximum(code - 1, 0) & 255) == block_iota)
        totals = totals + jnp.where(live, got, 0.0)
    for b in range(NB):
        for h in range(BLK // 128):
            out[b * (BLK // 128) + h : b * (BLK // 128) + h + 1, :] = totals[b : b + 1, h * 128 : (h + 1) * 128]

    for copy in r_copies[1:] + list(x_copies.values()):
        copy.wait_send()
    for j in range(1, J):
        for copy in [c_copies[j], i_copies[j]] + [a_copies[j, dl] for dl in order]:
            copy.wait_send()

    @pl.when(r != 0)
    def _():
        for copy in [r_copies[0], c_copies[0], i_copies[0]] + [a_copies[0, dl] for dl in order]:
            copy.wait_send()


def on_device(sizes, features, pair_list, pair_count):
    N, L, R = sizes
    rows = features.shape[0]
    blocks = features.reshape(rows // BLK, BLK, -1)
    NB, _, width = blocks.shape
    J = N // R
    HB = BLK // L
    table_rows = -(-N // 8) * 8
    dma = pltpu.SemaphoreType.DMA
    vmem = pl.BlockSpec(memory_space=pltpu.VMEM)
    smem = pl.BlockSpec(memory_space=pltpu.SMEM)
    totals = pl.pallas_call(
        functools.partial(body, N, L, R),
        out_shape=jax.ShapeDtypeStruct((rows // 128, 128), jnp.float32),
        in_specs=[vmem, smem, smem],
        out_specs=vmem,
        scratch_shapes=[
            pltpu.VMEM((R, table_rows, 128), jnp.int32),
            pltpu.VMEM((J, BLK, width), jnp.bfloat16),
            pltpu.VMEM((J, BLK, width), jnp.bfloat16),
            pltpu.VMEM((J, 8, 128), jnp.int32),
            pltpu.VMEM((J, 8, 128), jnp.int32),
            pltpu.VMEM((L, NB, BLK), jnp.float32),
            pltpu.VMEM((J, 1, BLK), jnp.float32),
            pltpu.VMEM((J, 1, BLK), jnp.float32),
            pltpu.VMEM((J, L - 1, HB, BLK), jnp.bfloat16),
            pltpu.VMEM((J, L - 1, HB, BLK), jnp.bfloat16),
            pltpu.VMEM((J, 1, BLK), jnp.float32),
            pltpu.VMEM((N * L, 1, BLK), jnp.float32),
            pltpu.VMEM((L * R, NB, BLK), jnp.float32),
            dma((R - 1,)), dma((R - 1,)),
            dma((J, L)), dma((J, L)),
            dma((J,)), dma((J,)),
            dma((L - 1,)), dma((L - 1,)),
            dma((J,)), dma((J,)),
            dma((J, L - 1)), dma((J, L - 1)),
            dma((J, L * R)), dma((N * L,)),
            dma((L * R - 1,)), dma((L * R - 1,)),
        ],
        compiler_params=pltpu.CompilerParams(
            collective_id=0, has_side_effects=True, vmem_limit_bytes=48 * 1024 * 1024
        ),
    )(blocks, pair_list.transpose(1, 2, 0), pair_count)
    return jnp.log1p(totals / BLK).reshape(-1)


def solution(mesh):
    sizes = (mesh.shape["ex"], mesh.shape["layer"], mesh.shape["rep"])
    return jax.shard_map(
        functools.partial(on_device, sizes),
        mesh=mesh,
        in_specs=(
            P(("groups", "ex"), "layer", None),
            P(None, ("groups", "ex"), "rep"),
            P(("groups", "ex"), "rep"),
        ),
        out_specs=P(("groups", "ex")),
        check_vma=False,
    )
```

```python
import functools

import jax
import jax.numpy as jnp
from jax import lax
from jax.experimental import pallas as pl
from jax.experimental.pallas import tpu as pltpu
from jax.sharding import PartitionSpec as P

BLK = 256
MESH = pl.DeviceIdType.MESH
CONTRACT_LAST = (((1,), (1,)), ((), ()))


def body(N, L, R, feat, plist, pcount, out, tab, stage, arow, csend, crecv, sq, isend, irecv, xsend, xrecv,
         rsend, rrecv, ctab, tab_s, tab_r, a_s, a_r, c_s, c_r, q_s, q_r, i_s, i_r, x_s, x_r, r_s, r_r, t_s, t_r):
    NB = feat.shape[0]
    slots = plist.shape[1]
    J = N // R
    HB = BLK // L
    e, l, r = lax.axis_index("ex"), lax.axis_index("layer"), lax.axis_index("rep")

    def place(d, dl, dr):
        return {"ex": lax.rem(e + d, N), "layer": lax.rem(l + dl, L), "rep": lax.rem(r + dr, R)}

    def remote(src, dst, ss, rs, target):
        return pltpu.make_async_remote_copy(
            src_ref=src, dst_ref=dst, send_sem=ss, recv_sem=rs, device_id=target, device_id_type=MESH
        )

    barrier = pltpu.get_barrier_semaphore()

    def greet(d, dl, dr):
        pl.semaphore_signal(barrier, inc=1, device_id=place(d, dl, dr), device_id_type=MESH)

    for j in reversed(range(J)):
        d = R * j + r
        if j == 0:

            @pl.when(r != 0)
            def _():
                greet(r, 0, 0)

        else:
            greet(d, 0, 0)
    for k in range(1, L * R):
        greet(0, k // R, k % R)

    rows_iota = lax.broadcasted_iota(jnp.int32, tab.shape[1:], 0)
    table = jnp.zeros(tab.shape[1:], jnp.int32)
    count = pcount[0, 0]
    for s in range(slots):
        code = jnp.where(s < count, 1 + plist[0, s, 0] + 256 * plist[0, s, 2], 0)
        table = table + jnp.where(rows_iota == plist[0, s, 1], code, 0)
    tab[r] = table

    ones = jnp.ones((8, feat.shape[2]), jnp.bfloat16)
    for b in range(NB):
        x = feat[b].astype(jnp.float32)
        x2 = x * x
        high = x2.astype(jnp.bfloat16)
        low = (x2 - high.astype(jnp.float32)).astype(jnp.bfloat16)
        s2 = lax.dot_general(ones, high, CONTRACT_LAST, preferred_element_type=jnp.float32)
        s2 = s2 + lax.dot_general(ones, low, CONTRACT_LAST, preferred_element_type=jnp.float32)
        sq[l, b : b + 1, :] = s2[0:1, :]

    pl.semaphore_wait(barrier, J - 1 + jnp.minimum(r, 1) + L * R - 1)


    tab_copies = []
    for dr in range(1, R):
        copy = remote(tab.at[r], tab.at[r], tab_s.at[dr - 1], tab_r.at[dr - 1], place(0, 0, dr))
        copy.start()
        tab_copies.append(copy)

    q_copies = []
    for dl in range(1, L):
        copy = remote(sq.at[l], sq.at[l], q_s.at[dl - 1], q_r.at[dl - 1], place(0, dl, 0))
        copy.start()
        q_copies.append(copy)

    for copy in tab_copies:
        copy.wait()
    table = tab[0]
    for i in range(1, R):
        table = table + tab[i]

    def part_rows(dl):
        return pl.ds(pl.multiple_of(lax.rem(l + dl, L) * HB, HB), HB)

    order = list(range(1, L)) + [0]
    codes, c_copies = [], []
    a_copies = {}
    for j in range(J):
        p = lax.rem(e + R * j + r, N)
        code = jnp.max(jnp.where(rows_iota == p, table, 0))
        codes.append(code)
        mine = jnp.maximum(code - 1, 0) & 255
        stage[j] = feat[mine]
        csend[j] = jnp.full(csend.shape[1:], code, jnp.int32)
        target = {"ex": p}
        c_copy = remote(csend.at[j], crecv.at[j], c_s.at[j], c_r.at[j], target)
        c_copies.append(c_copy)
        for dl in order:
            a_copies[j, dl] = remote(
                stage.at[j, part_rows(dl)], arow.at[j, part_rows(dl)], a_s.at[j, dl], a_r.at[j, dl], target
            )
        if j == 0:

            @pl.when(r == 0)
            def _():
                arow[0] = stage[0]
                crecv[0] = csend[0]

            @pl.when(r != 0)
            def _():
                c_copy.start()
                for dl in order[:-1]:
                    a_copies[0, dl].start()

        else:
            c_copy.start()
            for dl in order[:-1]:
                a_copies[j, dl].start()
    for j in range(J):
        if j == 0:

            @pl.when(r != 0)
            def _():
                a_copies[0, 0].start()

        else:
            a_copies[j, 0].start()

    for copy in q_copies:
        copy.wait()
    total_sq = sq[0]
    for i in range(1, L):
        total_sq = total_sq + sq[i]
    inv = lax.rsqrt(total_sq + 1e-06)

    i_copies = []
    for j in range(J):
        mine = jnp.maximum(codes[j] - 1, 0) & 255
        pick = jnp.zeros((1, BLK), jnp.float32)
        for b in range(NB):
            pick = jnp.where(mine == b, inv[b : b + 1, :], pick)
        isend[j] = pick
        copy = remote(isend.at[j], irecv.at[j], i_s.at[j], i_r.at[j], {"ex": lax.rem(e + R * j + r, N)})
        if j == 0:

            @pl.when(r == 0)
            def _():
                irecv[0] = isend[0]

            @pl.when(r != 0)
            def _():
                copy.start()

        else:
            copy.start()
        i_copies.append(copy)

    at_row = lax.broadcasted_iota(jnp.int32, (HB, BLK), 0) + l * HB
    at_column = lax.broadcasted_iota(jnp.int32, (HB, BLK), 1)
    spot = at_row == at_column
    columns = [jnp.zeros((1, BLK), jnp.float32) for _ in range(NB)]
    x_copies, rights = {}, []

    def arrived(j, *copies):
        if j == 0:

            @pl.when(r != 0)
            def _():
                for copy in copies:
                    copy.wait_recv()

        else:
            for copy in copies:
                copy.wait_recv()

    for j in range(J):
        arrived(j, c_copies[j])
        code = jnp.max(crecv[j])
        peer = jnp.maximum(code - 1, 0) // 256
        rights.append((code, peer))
        for dl in range(1, L):
            arrived(j, a_copies[j, dl])
            part = lax.dot_general(
                arow[j, part_rows(dl), :], feat[peer], CONTRACT_LAST, preferred_element_type=jnp.float32
            )
            xsend[j, dl - 1] = part.astype(jnp.bfloat16)
            copy = remote(
                xsend.at[j, dl - 1], xrecv.at[j, dl - 1], x_s.at[j, dl - 1], x_r.at[j, dl - 1], place(0, dl, 0)
            )
            copy.start()
            x_copies[j, dl] = copy

    r_copies = []
    for j in range(J):
        arrived(j, a_copies[j, 0], i_copies[j])
        dots = lax.dot_general(
            arow[j, part_rows(0), :], feat[rights[j][1]], CONTRACT_LAST, preferred_element_type=jnp.float32
        )
        for dl in range(1, L):
            x_copies[j, dl].wait_recv()
            dots = dots + xrecv[j, dl - 1].astype(jnp.float32)
        code, peer = rights[j]
        inv_row = jnp.sum(jnp.where(spot, irecv[j], 0.0), axis=1, keepdims=True)
        inv_column = jnp.zeros((1, BLK), jnp.float32)
        for b in range(NB):
            inv_column = jnp.where(peer == b, inv[b : b + 1, :], inv_column)
        kern = jnp.exp(20.0 * (dots * inv_row * inv_column))
        if j == 0:
            same = (r == 0) & ((jnp.maximum(code - 1, 0) & 255) == peer)
            kern = jnp.where(spot, kern * jnp.where(same, 0.0, 1.0), kern)
        row_sums = jnp.sum(kern, axis=1, keepdims=True)
        rsend[j] = jnp.sum(jnp.where(spot, row_sums, 0.0), axis=0, keepdims=True)
        column_sums = jnp.sum(kern, axis=0, keepdims=True)
        for b in range(NB):
            columns[b] = columns[b] + jnp.where((peer == b) & (code > 0), column_sums, 0.0)
        slot = e * L + l
        back = N - (R * j + r)
        for dl in range(L):
            for dr in range(R):
                k = dl * R + dr
                copy = remote(rsend.at[j], rrecv.at[slot], r_s.at[j, k], r_r.at[slot], place(back, dl, dr))
                if j == 0 and k == 0:

                    @pl.when(r == 0)
                    def _():
                        rrecv[slot] = rsend[0]

                    @pl.when(r != 0)
                    def _():
                        copy.start()

                else:
                    copy.start()
                r_copies.append(copy)

    mine_slot = l * R + r
    for b in range(NB):
        ctab[mine_slot, b : b + 1, :] = columns[b]
    t_copies = []
    for k in range(1, L * R):
        copy = remote(
            ctab.at[mine_slot], ctab.at[mine_slot], t_s.at[k - 1], t_r.at[k - 1], place(0, k // R, k % R)
        )
        copy.start()
        t_copies.append(copy)

    for k in range(1, L * R):
        t_copies[k - 1].wait()
    for d in range(N):
        p = lax.rem(e + d, N)
        for dl in range(L):
            slot = p * L + lax.rem(l + dl, L)
            copy = remote(rsend.at[0], rrecv.at[slot], r_s.at[0, 0], r_r.at[slot], place(0, 0, 1))
            if d == 0 and dl == 0:

                @pl.when(r != 0)
                def _():
                    copy.wait_recv()

            else:
                copy.wait_recv()

    totals = ctab[0]
    for i in range(1, L * R):
        totals = totals + ctab[i]
    block_iota = lax.broadcasted_iota(jnp.int32, (NB, BLK), 0)
    for p in range(N):
        got = rrecv[p * L]
        for i in range(1, L):
            got = got + rrecv[p * L + i]
        code = table[p : p + 1, :]
        code = jnp.concatenate([code] * (BLK // 128), axis=1)
        live = (code > 0) & ((jnp.maximum(code - 1, 0) & 255) == block_iota)
        totals = totals + jnp.where(live, got, 0.0)
    for b in range(NB):
        for h in range(BLK // 128):
            out[b * (BLK // 128) + h : b * (BLK // 128) + h + 1, :] = totals[b : b + 1, h * 128 : (h + 1) * 128]

    for copy in r_copies[1:] + list(x_copies.values()):
        copy.wait_send()
    for j in range(1, J):
        for copy in [c_copies[j], i_copies[j]] + [a_copies[j, dl] for dl in order]:
            copy.wait_send()

    @pl.when(r != 0)
    def _():
        for copy in [r_copies[0], c_copies[0], i_copies[0]] + [a_copies[0, dl] for dl in order]:
            copy.wait_send()


def on_device(sizes, features, pair_list, pair_count):
    N, L, R = sizes
    rows = features.shape[0]
    blocks = features.reshape(rows // BLK, BLK, -1)
    NB, _, width = blocks.shape
    J = N // R
    HB = BLK // L
    table_rows = -(-N // 8) * 8
    dma = pltpu.SemaphoreType.DMA
    vmem = pl.BlockSpec(memory_space=pltpu.VMEM)
    smem = pl.BlockSpec(memory_space=pltpu.SMEM)
    totals = pl.pallas_call(
        functools.partial(body, N, L, R),
        out_shape=jax.ShapeDtypeStruct((rows // 128, 128), jnp.float32),
        in_specs=[vmem, smem, smem],
        out_specs=vmem,
        scratch_shapes=[
            pltpu.VMEM((R, table_rows, 128), jnp.int32),
            pltpu.VMEM((J, BLK, width), jnp.bfloat16),
            pltpu.VMEM((J, BLK, width), jnp.bfloat16),
            pltpu.VMEM((J, 8, 128), jnp.int32),
            pltpu.VMEM((J, 8, 128), jnp.int32),
            pltpu.VMEM((L, NB, BLK), jnp.float32),
            pltpu.VMEM((J, 1, BLK), jnp.float32),
            pltpu.VMEM((J, 1, BLK), jnp.float32),
            pltpu.VMEM((J, L - 1, HB, BLK), jnp.bfloat16),
            pltpu.VMEM((J, L - 1, HB, BLK), jnp.bfloat16),
            pltpu.VMEM((J, 1, BLK), jnp.float32),
            pltpu.VMEM((N * L, 1, BLK), jnp.float32),
            pltpu.VMEM((L * R, NB, BLK), jnp.float32),
            dma((R - 1,)), dma((R - 1,)),
            dma((J, L)), dma((J, L)),
            dma((J,)), dma((J,)),
            dma((L - 1,)), dma((L - 1,)),
            dma((J,)), dma((J,)),
            dma((J, L - 1)), dma((J, L - 1)),
            dma((J, L * R)), dma((N * L,)),
            dma((L * R - 1,)), dma((L * R - 1,)),
        ],
        compiler_params=pltpu.CompilerParams(
            collective_id=0, has_side_effects=True, vmem_limit_bytes=48 * 1024 * 1024
        ),
    )(blocks, pair_list.transpose(1, 2, 0), pair_count)
    return jnp.log1p(totals / BLK).reshape(-1)


def solution(mesh):
    sizes = (mesh.shape["ex"], mesh.shape["layer"], mesh.shape["rep"])
    return jax.shard_map(
        functools.partial(on_device, sizes),
        mesh=mesh,
        in_specs=(
            P(("groups", "ex"), "layer", None),
            P(None, ("groups", "ex"), "rep"),
            P(("groups", "ex"), "rep"),
        ),
        out_specs=P(("groups", "ex")),
        check_vma=False,
    )
```

```python
import functools

import jax
import jax.numpy as jnp
from jax import lax
from jax.experimental import pallas as pl
from jax.experimental.pallas import tpu as pltpu
from jax.sharding import PartitionSpec as P

BLK = 256
MESH = pl.DeviceIdType.MESH
CONTRACT_LAST = (((1,), (1,)), ((), ()))


def body(N, L, R, feat, plist, pcount, out, tab, stage, arow, csend, crecv, sq, isend, irecv, xsend, xrecv,
         rsend, rrecv, ctab, scale, tab_s, tab_r, a_s, a_r, c_s, c_r, q_s, q_r, i_s, i_r, x_s, x_r, r_s, r_r, t_s, t_r):
    NB = feat.shape[0]
    slots = plist.shape[1]
    J = N // R
    HB = BLK // L
    e, l, r = lax.axis_index("ex"), lax.axis_index("layer"), lax.axis_index("rep")

    def place(d, dl, dr):
        return {"ex": lax.rem(e + d, N), "layer": lax.rem(l + dl, L), "rep": lax.rem(r + dr, R)}

    def remote(src, dst, ss, rs, target):
        return pltpu.make_async_remote_copy(
            src_ref=src, dst_ref=dst, send_sem=ss, recv_sem=rs, device_id=target, device_id_type=MESH
        )

    barrier = pltpu.get_barrier_semaphore()

    def greet(d, dl, dr):
        pl.semaphore_signal(barrier, inc=1, device_id=place(d, dl, dr), device_id_type=MESH)

    for j in reversed(range(J)):
        d = R * j + r
        if j == 0:

            @pl.when(r != 0)
            def _():
                greet(r, 0, 0)

        else:
            greet(d, 0, 0)
    for k in range(1, L * R):
        greet(0, k // R, k % R)

    rows_iota = lax.broadcasted_iota(jnp.int32, tab.shape[1:], 0)
    table = jnp.zeros(tab.shape[1:], jnp.int32)
    count = pcount[0, 0]
    for s in range(slots):
        code = jnp.where(s < count, 1 + plist[0, s, 0] + 256 * plist[0, s, 2], 0)
        table = table + jnp.where(rows_iota == plist[0, s, 1], code, 0)
    tab[r] = table

    ones = jnp.ones((8, feat.shape[2]), jnp.bfloat16)
    for b in range(NB):
        x = feat[b].astype(jnp.float32)
        x2 = x * x
        high = x2.astype(jnp.bfloat16)
        low = (x2 - high.astype(jnp.float32)).astype(jnp.bfloat16)
        s2 = lax.dot_general(ones, high, CONTRACT_LAST, preferred_element_type=jnp.float32)
        s2 = s2 + lax.dot_general(ones, low, CONTRACT_LAST, preferred_element_type=jnp.float32)
        sq[l, b : b + 1, :] = s2[0:1, :]

    pl.semaphore_wait(barrier, J - 1 + jnp.minimum(r, 1) + L * R - 1)


    tab_copies = []
    for dr in range(1, R):
        copy = remote(tab.at[r], tab.at[r], tab_s.at[dr - 1], tab_r.at[dr - 1], place(0, 0, dr))
        copy.start()
        tab_copies.append(copy)

    q_copies = []
    for dl in range(1, L):
        copy = remote(sq.at[l], sq.at[l], q_s.at[dl - 1], q_r.at[dl - 1], place(0, dl, 0))
        copy.start()
        q_copies.append(copy)

    for copy in tab_copies:
        copy.wait()
    table = tab[0]
    for i in range(1, R):
        table = table + tab[i]

    def part_rows(dl):
        return pl.ds(pl.multiple_of(lax.rem(l + dl, L) * HB, HB), HB)

    order = list(range(1, L)) + [0]
    codes, c_copies = [], []
    a_copies = {}
    for j in range(J):
        p = lax.rem(e + R * j + r, N)
        code = jnp.max(jnp.where(rows_iota == p, table, 0))
        codes.append(code)
        mine = jnp.maximum(code - 1, 0) & 255
        stage[j] = feat[mine]
        csend[j] = jnp.full(csend.shape[1:], code, jnp.int32)
        target = {"ex": p}
        c_copy = remote(csend.at[j], crecv.at[j], c_s.at[j], c_r.at[j], target)
        c_copies.append(c_copy)
        for dl in order:
            a_copies[j, dl] = remote(
                stage.at[j, part_rows(dl)], arow.at[j, part_rows(dl)], a_s.at[j, dl], a_r.at[j, dl], target
            )
        if j == 0:

            @pl.when(r == 0)
            def _():
                arow[0] = stage[0]
                crecv[0] = csend[0]

            @pl.when(r != 0)
            def _():
                c_copy.start()
                for dl in order[:-1]:
                    a_copies[0, dl].start()

        else:
            c_copy.start()
            for dl in order[:-1]:
                a_copies[j, dl].start()
    for j in reversed(range(J)):
        if j == 0:

            @pl.when(r != 0)
            def _():
                a_copies[0, 0].start()

        else:
            a_copies[j, 0].start()

    for copy in q_copies:
        copy.wait()
    total_sq = sq[0]
    for i in range(1, L):
        total_sq = total_sq + sq[i]
    inv = lax.rsqrt(total_sq + 1e-06)

    i_copies = []
    for j in range(J):
        mine = jnp.maximum(codes[j] - 1, 0) & 255
        pick = jnp.zeros((1, BLK), jnp.float32)
        for b in range(NB):
            pick = jnp.where(mine == b, inv[b : b + 1, :], pick)
        isend[j] = pick
        copy = remote(isend.at[j], irecv.at[j], i_s.at[j], i_r.at[j], {"ex": lax.rem(e + R * j + r, N)})
        if j == 0:

            @pl.when(r == 0)
            def _():
                irecv[0] = isend[0]

            @pl.when(r != 0)
            def _():
                copy.start()

        else:
            copy.start()
        i_copies.append(copy)

    at_row = lax.broadcasted_iota(jnp.int32, (HB, BLK), 0) + l * HB
    at_column = lax.broadcasted_iota(jnp.int32, (HB, BLK), 1)
    spot = at_row == at_column
    columns = [jnp.zeros((1, BLK), jnp.float32) for _ in range(NB)]
    block_iota = lax.broadcasted_iota(jnp.int32, (NB, BLK), 0)
    held = []
    for p in range(N):
        code = jnp.concatenate([table[p : p + 1, :]] * (BLK // 128), axis=1)
        held.append((code > 0) & ((jnp.maximum(code - 1, 0) & 255) == block_iota))
    x_copies, rights = {}, []

    def arrived(j, *copies):
        if j == 0:

            @pl.when(r != 0)
            def _():
                for copy in copies:
                    copy.wait_recv()

        else:
            for copy in copies:
                copy.wait_recv()

    for j in range(J):
        arrived(j, c_copies[j])
        code = jnp.max(crecv[j])
        peer = jnp.maximum(code - 1, 0) // 256
        rights.append((code, peer))
        for dl in range(1, L):
            arrived(j, a_copies[j, dl])
            part = lax.dot_general(
                arow[j, part_rows(dl), :], feat[peer], CONTRACT_LAST, preferred_element_type=jnp.float32
            )
            xsend[j, dl - 1] = part.astype(jnp.bfloat16)
            copy = remote(
                xsend.at[j, dl - 1], xrecv.at[j, dl - 1], x_s.at[j, dl - 1], x_r.at[j, dl - 1], place(0, dl, 0)
            )
            copy.start()
            x_copies[j, dl] = copy

    for j in range(J):
        arrived(j, i_copies[j])
        inv_row = jnp.sum(jnp.where(spot, irecv[j], 0.0), axis=1, keepdims=True)
        inv_column = jnp.zeros((1, BLK), jnp.float32)
        for b in range(NB):
            inv_column = jnp.where(rights[j][1] == b, inv[b : b + 1, :], inv_column)
        scale[j] = 20.0 * (inv_row * inv_column)

    r_copies = []
    for j in range(J):
        arrived(j, a_copies[j, 0])
        dots = lax.dot_general(
            arow[j, part_rows(0), :], feat[rights[j][1]], CONTRACT_LAST, preferred_element_type=jnp.float32
        )
        for dl in range(1, L):
            x_copies[j, dl].wait_recv()
            dots = dots + xrecv[j, dl - 1].astype(jnp.float32)
        code, peer = rights[j]
        kern = jnp.exp(dots * scale[j])
        if j == 0:
            same = (r == 0) & ((jnp.maximum(code - 1, 0) & 255) == peer)
            kern = jnp.where(spot, kern * jnp.where(same, 0.0, 1.0), kern)
        row_sums = jnp.sum(kern, axis=1, keepdims=True)
        rsend[j] = jnp.sum(jnp.where(spot, row_sums, 0.0), axis=0, keepdims=True)
        column_sums = jnp.sum(kern, axis=0, keepdims=True)
        for b in range(NB):
            columns[b] = columns[b] + jnp.where((peer == b) & (code > 0), column_sums, 0.0)
        slot = e * L + l
        back = N - (R * j + r)
        for dl in range(L):
            for dr in range(R):
                k = dl * R + dr
                copy = remote(rsend.at[j], rrecv.at[slot], r_s.at[j, k], r_r.at[slot], place(back, dl, dr))
                if j == 0 and k == 0:

                    @pl.when(r == 0)
                    def _():
                        rrecv[slot] = rsend[0]

                    @pl.when(r != 0)
                    def _():
                        copy.start()

                else:
                    copy.start()
                r_copies.append(copy)

    mine_slot = l * R + r
    for b in range(NB):
        ctab[mine_slot, b : b + 1, :] = columns[b]
    t_copies = []
    for k in range(1, L * R):
        copy = remote(
            ctab.at[mine_slot], ctab.at[mine_slot], t_s.at[k - 1], t_r.at[k - 1], place(0, k // R, k % R)
        )
        copy.start()
        t_copies.append(copy)

    for k in range(1, L * R):
        t_copies[k - 1].wait()
    for d in range(N):
        p = lax.rem(e + d, N)
        for dl in range(L):
            slot = p * L + lax.rem(l + dl, L)
            copy = remote(rsend.at[0], rrecv.at[slot], r_s.at[0, 0], r_r.at[slot], place(0, 0, 1))
            if d == 0 and dl == 0:

                @pl.when(r != 0)
                def _():
                    copy.wait_recv()

            else:
                copy.wait_recv()

    totals = ctab[0]
    for i in range(1, L * R):
        totals = totals + ctab[i]
    for p in range(N):
        got = rrecv[p * L]
        for i in range(1, L):
            got = got + rrecv[p * L + i]
        totals = totals + jnp.where(held[p], got, 0.0)
    for b in range(NB):
        for h in range(BLK // 128):
            out[b * (BLK // 128) + h : b * (BLK // 128) + h + 1, :] = totals[b : b + 1, h * 128 : (h + 1) * 128]

    for copy in r_copies[1:] + list(x_copies.values()):
        copy.wait_send()
    for j in range(1, J):
        for copy in [c_copies[j], i_copies[j]] + [a_copies[j, dl] for dl in order]:
            copy.wait_send()

    @pl.when(r != 0)
    def _():
        for copy in [r_copies[0], c_copies[0], i_copies[0]] + [a_copies[0, dl] for dl in order]:
            copy.wait_send()


def on_device(sizes, features, pair_list, pair_count):
    N, L, R = sizes
    rows = features.shape[0]
    blocks = features.reshape(rows // BLK, BLK, -1)
    NB, _, width = blocks.shape
    J = N // R
    HB = BLK // L
    table_rows = -(-N // 8) * 8
    dma = pltpu.SemaphoreType.DMA
    vmem = pl.BlockSpec(memory_space=pltpu.VMEM)
    smem = pl.BlockSpec(memory_space=pltpu.SMEM)
    totals = pl.pallas_call(
        functools.partial(body, N, L, R),
        out_shape=jax.ShapeDtypeStruct((rows // 128, 128), jnp.float32),
        in_specs=[vmem, smem, smem],
        out_specs=vmem,
        scratch_shapes=[
            pltpu.VMEM((R, table_rows, 128), jnp.int32),
            pltpu.VMEM((J, BLK, width), jnp.bfloat16),
            pltpu.VMEM((J, BLK, width), jnp.bfloat16),
            pltpu.VMEM((J, 8, 128), jnp.int32),
            pltpu.VMEM((J, 8, 128), jnp.int32),
            pltpu.VMEM((L, NB, BLK), jnp.float32),
            pltpu.VMEM((J, 1, BLK), jnp.float32),
            pltpu.VMEM((J, 1, BLK), jnp.float32),
            pltpu.VMEM((J, L - 1, HB, BLK), jnp.bfloat16),
            pltpu.VMEM((J, L - 1, HB, BLK), jnp.bfloat16),
            pltpu.VMEM((J, 1, BLK), jnp.float32),
            pltpu.VMEM((N * L, 1, BLK), jnp.float32),
            pltpu.VMEM((L * R, NB, BLK), jnp.float32),
            pltpu.VMEM((J, HB, BLK), jnp.float32),
            dma((R - 1,)), dma((R - 1,)),
            dma((J, L)), dma((J, L)),
            dma((J,)), dma((J,)),
            dma((L - 1,)), dma((L - 1,)),
            dma((J,)), dma((J,)),
            dma((J, L - 1)), dma((J, L - 1)),
            dma((J, L * R)), dma((N * L,)),
            dma((L * R - 1,)), dma((L * R - 1,)),
        ],
        compiler_params=pltpu.CompilerParams(
            collective_id=0, has_side_effects=True, vmem_limit_bytes=48 * 1024 * 1024
        ),
    )(blocks, pair_list.transpose(1, 2, 0), pair_count)
    return jnp.log1p(totals / BLK).reshape(-1)


def solution(mesh):
    sizes = (mesh.shape["ex"], mesh.shape["layer"], mesh.shape["rep"])
    return jax.shard_map(
        functools.partial(on_device, sizes),
        mesh=mesh,
        in_specs=(
            P(("groups", "ex"), "layer", None),
            P(None, ("groups", "ex"), "rep"),
            P(("groups", "ex"), "rep"),
        ),
        out_specs=P(("groups", "ex")),
        check_vma=False,
    )
```

```python
import functools

import jax
import jax.numpy as jnp
from jax import lax
from jax.experimental import pallas as pl
from jax.experimental.pallas import tpu as pltpu
from jax.sharding import PartitionSpec as P

BLK = 256
MESH = pl.DeviceIdType.MESH
CONTRACT_LAST = (((1,), (1,)), ((), ()))


def body(N, L, R, feat, plist, pcount, out, tab, stage, arow, csend, crecv, sq, isend, irecv, xsend, xrecv,
         rsend, rrecv, ctab, scale, tab_s, tab_r, a_s, a_r, c_s, c_r, q_s, q_r, i_s, i_r, x_s, x_r, r_s, r_r, t_s, t_r):
    NB = feat.shape[0]
    slots = plist.shape[1]
    J = N // R
    HB = BLK // L
    e, l, r = lax.axis_index("ex"), lax.axis_index("layer"), lax.axis_index("rep")

    def place(d, dl, dr):
        return {"ex": lax.rem(e + d, N), "layer": lax.rem(l + dl, L), "rep": lax.rem(r + dr, R)}

    def remote(src, dst, ss, rs, target):
        return pltpu.make_async_remote_copy(
            src_ref=src, dst_ref=dst, send_sem=ss, recv_sem=rs, device_id=target, device_id_type=MESH
        )

    barrier = pltpu.get_barrier_semaphore()

    def greet(d, dl, dr):
        pl.semaphore_signal(barrier, inc=1, device_id=place(d, dl, dr), device_id_type=MESH)

    for j in reversed(range(J)):
        d = R * j + r
        if j == 0:

            @pl.when(r != 0)
            def _():
                greet(r, 0, 0)

        else:
            greet(d, 0, 0)
    for k in range(1, L * R):
        greet(0, k // R, k % R)

    rows_iota = lax.broadcasted_iota(jnp.int32, tab.shape[1:], 0)
    table = jnp.zeros(tab.shape[1:], jnp.int32)
    count = pcount[0, 0]
    for s in range(slots):
        code = jnp.where(s < count, 1 + plist[0, s, 0] + 256 * plist[0, s, 2], 0)
        table = table + jnp.where(rows_iota == plist[0, s, 1], code, 0)
    tab[r] = table

    ones = jnp.ones((8, feat.shape[2]), jnp.bfloat16)
    for b in range(NB):
        x = feat[b].astype(jnp.float32)
        x2 = x * x
        high = x2.astype(jnp.bfloat16)
        low = (x2 - high.astype(jnp.float32)).astype(jnp.bfloat16)
        s2 = lax.dot_general(ones, high, CONTRACT_LAST, preferred_element_type=jnp.float32)
        s2 = s2 + lax.dot_general(ones, low, CONTRACT_LAST, preferred_element_type=jnp.float32)
        sq[l, b : b + 1, :] = s2[0:1, :]

    pl.semaphore_wait(barrier, J - 1 + jnp.minimum(r, 1) + L * R - 1)


    tab_copies = []
    for dr in range(1, R):
        copy = remote(tab.at[r], tab.at[r], tab_s.at[dr - 1], tab_r.at[dr - 1], place(0, 0, dr))
        copy.start()
        tab_copies.append(copy)

    q_copies = []
    for dl in range(1, L):
        copy = remote(sq.at[l], sq.at[l], q_s.at[dl - 1], q_r.at[dl - 1], place(0, dl, 0))
        copy.start()
        q_copies.append(copy)

    for copy in tab_copies:
        copy.wait()
    table = tab[0]
    for i in range(1, R):
        table = table + tab[i]

    def part_rows(dl):
        return pl.ds(pl.multiple_of(lax.rem(l + dl, L) * HB, HB), HB)

    order = list(range(1, L)) + [0]
    codes, c_copies, a_copies = {}, {}, {}
    for j in reversed(range(J)):
        p = lax.rem(e + R * j + r, N)
        code = jnp.max(jnp.where(rows_iota == p, table, 0))
        codes[j] = code
        mine = jnp.maximum(code - 1, 0) & 255
        stage[j] = feat[mine]
        csend[j] = jnp.full(csend.shape[1:], code, jnp.int32)
        target = {"ex": p}
        c_copy = remote(csend.at[j], crecv.at[j], c_s.at[j], c_r.at[j], target)
        c_copies[j] = c_copy
        for dl in order:
            a_copies[j, dl] = remote(
                stage.at[j, part_rows(dl)], arow.at[j, part_rows(dl)], a_s.at[j, dl], a_r.at[j, dl], target
            )
        if j == 0:

            @pl.when(r == 0)
            def _():
                arow[0] = stage[0]
                crecv[0] = csend[0]

            @pl.when(r != 0)
            def _():
                c_copy.start()
                for dl in order[:-1]:
                    a_copies[0, dl].start()

        else:
            c_copy.start()
            for dl in order[:-1]:
                a_copies[j, dl].start()
    for j in reversed(range(J)):
        if j == 0:

            @pl.when(r != 0)
            def _():
                a_copies[0, 0].start()

        else:
            a_copies[j, 0].start()

    for copy in q_copies:
        copy.wait()
    total_sq = sq[0]
    for i in range(1, L):
        total_sq = total_sq + sq[i]
    inv = lax.rsqrt(total_sq + 1e-06)

    i_copies = []
    for j in range(J):
        mine = jnp.maximum(codes[j] - 1, 0) & 255
        pick = jnp.zeros((1, BLK), jnp.float32)
        for b in range(NB):
            pick = jnp.where(mine == b, inv[b : b + 1, :], pick)
        isend[j] = pick
        copy = remote(isend.at[j], irecv.at[j], i_s.at[j], i_r.at[j], {"ex": lax.rem(e + R * j + r, N)})
        if j == 0:

            @pl.when(r == 0)
            def _():
                irecv[0] = isend[0]

            @pl.when(r != 0)
            def _():
                copy.start()

        else:
            copy.start()
        i_copies.append(copy)

    at_row = lax.broadcasted_iota(jnp.int32, (HB, BLK), 0) + l * HB
    at_column = lax.broadcasted_iota(jnp.int32, (HB, BLK), 1)
    spot = at_row == at_column
    columns = [jnp.zeros((1, BLK), jnp.float32) for _ in range(NB)]
    block_iota = lax.broadcasted_iota(jnp.int32, (NB, BLK), 0)
    held = []
    for p in range(N):
        code = jnp.concatenate([table[p : p + 1, :]] * (BLK // 128), axis=1)
        held.append((code > 0) & ((jnp.maximum(code - 1, 0) & 255) == block_iota))
    x_copies, rights = {}, []

    def arrived(j, *copies):
        if j == 0:

            @pl.when(r != 0)
            def _():
                for copy in copies:
                    copy.wait_recv()

        else:
            for copy in copies:
                copy.wait_recv()

    for j in range(J):
        arrived(j, c_copies[j])
        code = jnp.max(crecv[j])
        peer = jnp.maximum(code - 1, 0) // 256
        rights.append((code, peer))
        for dl in range(1, L):
            arrived(j, a_copies[j, dl])
            part = lax.dot_general(
                arow[j, part_rows(dl), :], feat[peer], CONTRACT_LAST, preferred_element_type=jnp.float32
            )
            xsend[j, dl - 1] = part.astype(jnp.bfloat16)
            copy = remote(
                xsend.at[j, dl - 1], xrecv.at[j, dl - 1], x_s.at[j, dl - 1], x_r.at[j, dl - 1], place(0, dl, 0)
            )
            copy.start()
            x_copies[j, dl] = copy

    for j in range(J):
        arrived(j, i_copies[j])
        inv_row = jnp.sum(jnp.where(spot, irecv[j], 0.0), axis=1, keepdims=True)
        inv_column = jnp.zeros((1, BLK), jnp.float32)
        for b in range(NB):
            inv_column = jnp.where(rights[j][1] == b, inv[b : b + 1, :], inv_column)
        scale[j] = 20.0 * (inv_row * inv_column)

    r_copies = []
    for j in range(J):
        arrived(j, a_copies[j, 0])
        dots = lax.dot_general(
            arow[j, part_rows(0), :], feat[rights[j][1]], CONTRACT_LAST, preferred_element_type=jnp.float32
        )
        for dl in range(1, L):
            x_copies[j, dl].wait_recv()
            dots = dots + xrecv[j, dl - 1].astype(jnp.float32)
        code, peer = rights[j]
        kern = jnp.exp(dots * scale[j])
        if j == 0:
            same = (r == 0) & ((jnp.maximum(code - 1, 0) & 255) == peer)
            kern = jnp.where(spot, kern * jnp.where(same, 0.0, 1.0), kern)
        row_sums = jnp.sum(kern, axis=1, keepdims=True)
        rsend[j] = jnp.sum(jnp.where(spot, row_sums, 0.0), axis=0, keepdims=True)
        column_sums = jnp.sum(kern, axis=0, keepdims=True)
        for b in range(NB):
            columns[b] = columns[b] + jnp.where((peer == b) & (code > 0), column_sums, 0.0)
        slot = e * L + l
        back = N - (R * j + r)
        for dl in range(L):
            for dr in range(R):
                k = dl * R + dr
                copy = remote(rsend.at[j], rrecv.at[slot], r_s.at[j, k], r_r.at[slot], place(back, dl, dr))
                if j == 0 and k == 0:

                    @pl.when(r == 0)
                    def _():
                        rrecv[slot] = rsend[0]

                    @pl.when(r != 0)
                    def _():
                        copy.start()

                else:
                    copy.start()
                r_copies.append(copy)

    mine_slot = l * R + r
    for b in range(NB):
        ctab[mine_slot, b : b + 1, :] = columns[b]
    t_copies = []
    for k in range(1, L * R):
        copy = remote(
            ctab.at[mine_slot], ctab.at[mine_slot], t_s.at[k - 1], t_r.at[k - 1], place(0, k // R, k % R)
        )
        copy.start()
        t_copies.append(copy)

    for k in range(1, L * R):
        t_copies[k - 1].wait()
    for d in range(N):
        p = lax.rem(e + d, N)
        for dl in range(L):
            slot = p * L + lax.rem(l + dl, L)
            copy = remote(rsend.at[0], rrecv.at[slot], r_s.at[0, 0], r_r.at[slot], place(0, 0, 1))
            if d == 0 and dl == 0:

                @pl.when(r != 0)
                def _():
                    copy.wait_recv()

            else:
                copy.wait_recv()

    totals = ctab[0]
    for i in range(1, L * R):
        totals = totals + ctab[i]
    for p in range(N):
        got = rrecv[p * L]
        for i in range(1, L):
            got = got + rrecv[p * L + i]
        totals = totals + jnp.where(held[p], got, 0.0)
    for b in range(NB):
        for h in range(BLK // 128):
            out[b * (BLK // 128) + h : b * (BLK // 128) + h + 1, :] = totals[b : b + 1, h * 128 : (h + 1) * 128]

    for copy in r_copies[1:] + list(x_copies.values()):
        copy.wait_send()
    for j in range(1, J):
        for copy in [c_copies[j], i_copies[j]] + [a_copies[j, dl] for dl in order]:
            copy.wait_send()

    @pl.when(r != 0)
    def _():
        for copy in [r_copies[0], c_copies[0], i_copies[0]] + [a_copies[0, dl] for dl in order]:
            copy.wait_send()


def on_device(sizes, features, pair_list, pair_count):
    N, L, R = sizes
    rows = features.shape[0]
    blocks = features.reshape(rows // BLK, BLK, -1)
    NB, _, width = blocks.shape
    J = N // R
    HB = BLK // L
    table_rows = -(-N // 8) * 8
    dma = pltpu.SemaphoreType.DMA
    vmem = pl.BlockSpec(memory_space=pltpu.VMEM)
    smem = pl.BlockSpec(memory_space=pltpu.SMEM)
    totals = pl.pallas_call(
        functools.partial(body, N, L, R),
        out_shape=jax.ShapeDtypeStruct((rows // 128, 128), jnp.float32),
        in_specs=[vmem, smem, smem],
        out_specs=vmem,
        scratch_shapes=[
            pltpu.VMEM((R, table_rows, 128), jnp.int32),
            pltpu.VMEM((J, BLK, width), jnp.bfloat16),
            pltpu.VMEM((J, BLK, width), jnp.bfloat16),
            pltpu.VMEM((J, 8, 128), jnp.int32),
            pltpu.VMEM((J, 8, 128), jnp.int32),
            pltpu.VMEM((L, NB, BLK), jnp.float32),
            pltpu.VMEM((J, 1, BLK), jnp.float32),
            pltpu.VMEM((J, 1, BLK), jnp.float32),
            pltpu.VMEM((J, L - 1, HB, BLK), jnp.bfloat16),
            pltpu.VMEM((J, L - 1, HB, BLK), jnp.bfloat16),
            pltpu.VMEM((J, 1, BLK), jnp.float32),
            pltpu.VMEM((N * L, 1, BLK), jnp.float32),
            pltpu.VMEM((L * R, NB, BLK), jnp.float32),
            pltpu.VMEM((J, HB, BLK), jnp.float32),
            dma((R - 1,)), dma((R - 1,)),
            dma((J, L)), dma((J, L)),
            dma((J,)), dma((J,)),
            dma((L - 1,)), dma((L - 1,)),
            dma((J,)), dma((J,)),
            dma((J, L - 1)), dma((J, L - 1)),
            dma((J, L * R)), dma((N * L,)),
            dma((L * R - 1,)), dma((L * R - 1,)),
        ],
        compiler_params=pltpu.CompilerParams(
            collective_id=0, has_side_effects=True, vmem_limit_bytes=48 * 1024 * 1024
        ),
    )(blocks, pair_list.transpose(1, 2, 0), pair_count)
    return jnp.log1p(totals / BLK).reshape(-1)


def solution(mesh):
    sizes = (mesh.shape["ex"], mesh.shape["layer"], mesh.shape["rep"])
    return jax.shard_map(
        functools.partial(on_device, sizes),
        mesh=mesh,
        in_specs=(
            P(("groups", "ex"), "layer", None),
            P(None, ("groups", "ex"), "rep"),
            P(("groups", "ex"), "rep"),
        ),
        out_specs=P(("groups", "ex")),
        check_vma=False,
    )
```

```python
import functools

import jax
import jax.numpy as jnp
from jax import lax
from jax.experimental import pallas as pl
from jax.experimental.pallas import tpu as pltpu
from jax.sharding import PartitionSpec as P

BLK = 256
MESH = pl.DeviceIdType.MESH
CONTRACT_LAST = (((1,), (1,)), ((), ()))


def body(N, L, R, feat, plist, pcount, out, tab, stage, arow, csend, crecv, sq, isend, irecv, xsend, xrecv,
         rsend, rrecv, ctab, scale, tab_s, tab_r, a_s, a_r, c_s, c_r, q_s, q_r, i_s, i_r, x_s, x_r, r_s, r_r, t_s, t_r):
    NB = feat.shape[0]
    slots = plist.shape[1]
    J = N // R
    HB = BLK // L
    e, l, r = lax.axis_index("ex"), lax.axis_index("layer"), lax.axis_index("rep")

    def place(d, dl, dr):
        return {"ex": lax.rem(e + d, N), "layer": lax.rem(l + dl, L), "rep": lax.rem(r + dr, R)}

    def remote(src, dst, ss, rs, target):
        return pltpu.make_async_remote_copy(
            src_ref=src, dst_ref=dst, send_sem=ss, recv_sem=rs, device_id=target, device_id_type=MESH
        )

    barrier = pltpu.get_barrier_semaphore()

    def greet(d, dl, dr):
        pl.semaphore_signal(barrier, inc=1, device_id=place(d, dl, dr), device_id_type=MESH)

    for j in reversed(range(J)):
        d = R * j + r
        if j == 0:

            @pl.when(r != 0)
            def _():
                greet(r, 0, 0)

        else:
            greet(d, 0, 0)
    for k in range(1, L * R):
        greet(0, k // R, k % R)

    rows_iota = lax.broadcasted_iota(jnp.int32, tab.shape[1:], 0)
    table = jnp.zeros(tab.shape[1:], jnp.int32)
    count = pcount[0, 0]
    for s in range(slots):
        code = jnp.where(s < count, 1 + plist[0, s, 0] + 256 * plist[0, s, 2], 0)
        table = table + jnp.where(rows_iota == plist[0, s, 1], code, 0)
    tab[r] = table

    ones = jnp.ones((8, feat.shape[2]), jnp.bfloat16)
    for b in range(NB):
        x = feat[b].astype(jnp.float32)
        x2 = x * x
        high = x2.astype(jnp.bfloat16)
        low = (x2 - high.astype(jnp.float32)).astype(jnp.bfloat16)
        s2 = lax.dot_general(ones, high, CONTRACT_LAST, preferred_element_type=jnp.float32)
        s2 = s2 + lax.dot_general(ones, low, CONTRACT_LAST, preferred_element_type=jnp.float32)
        sq[l, b : b + 1, :] = s2[0:1, :]

    pl.semaphore_wait(barrier, J - 1 + jnp.minimum(r, 1) + L * R - 1)


    tab_copies = []
    for dr in range(1, R):
        copy = remote(tab.at[r], tab.at[r], tab_s.at[dr - 1], tab_r.at[dr - 1], place(0, 0, dr))
        copy.start()
        tab_copies.append(copy)

    q_copies = []
    for dl in range(1, L):
        copy = remote(sq.at[l], sq.at[l], q_s.at[dl - 1], q_r.at[dl - 1], place(0, dl, 0))
        copy.start()
        q_copies.append(copy)

    for copy in tab_copies:
        copy.wait()
    table = tab[0]
    for i in range(1, R):
        table = table + tab[i]

    def part_rows(dl):
        return pl.ds(pl.multiple_of(lax.rem(l + dl, L) * HB, HB), HB)

    order = list(range(1, L)) + [0]
    codes, c_copies, a_copies = {}, {}, {}
    for j in reversed(range(J)):
        p = lax.rem(e + R * j + r, N)
        code = jnp.max(jnp.where(rows_iota == p, table, 0))
        codes[j] = code
        mine = jnp.maximum(code - 1, 0) & 255
        for dl in order[:-1]:
            stage[j, part_rows(dl), :] = feat[mine, part_rows(dl), :]
        csend[j] = jnp.full(csend.shape[1:], code, jnp.int32)
        target = {"ex": p}
        c_copy = remote(csend.at[j], crecv.at[j], c_s.at[j], c_r.at[j], target)
        c_copies[j] = c_copy
        for dl in order:
            a_copies[j, dl] = remote(
                stage.at[j, part_rows(dl)], arow.at[j, part_rows(dl)], a_s.at[j, dl], a_r.at[j, dl], target
            )
        if j == 0:

            @pl.when(r == 0)
            def _():
                arow[0] = feat[mine]
                crecv[0] = csend[0]

            @pl.when(r != 0)
            def _():
                c_copy.start()
                for dl in order[:-1]:
                    a_copies[0, dl].start()

        else:
            c_copy.start()
            for dl in order[:-1]:
                a_copies[j, dl].start()
    for j in reversed(range(J)):
        mine = jnp.maximum(codes[j] - 1, 0) & 255
        stage[j, part_rows(0), :] = feat[mine, part_rows(0), :]
        if j == 0:

            @pl.when(r != 0)
            def _():
                a_copies[0, 0].start()

        else:
            a_copies[j, 0].start()

    for copy in q_copies:
        copy.wait()
    total_sq = sq[0]
    for i in range(1, L):
        total_sq = total_sq + sq[i]
    inv = lax.rsqrt(total_sq + 1e-06)

    i_copies = []
    for j in range(J):
        mine = jnp.maximum(codes[j] - 1, 0) & 255
        pick = jnp.zeros((1, BLK), jnp.float32)
        for b in range(NB):
            pick = jnp.where(mine == b, inv[b : b + 1, :], pick)
        isend[j] = pick
        copy = remote(isend.at[j], irecv.at[j], i_s.at[j], i_r.at[j], {"ex": lax.rem(e + R * j + r, N)})
        if j == 0:

            @pl.when(r == 0)
            def _():
                irecv[0] = isend[0]

            @pl.when(r != 0)
            def _():
                copy.start()

        else:
            copy.start()
        i_copies.append(copy)

    at_row = lax.broadcasted_iota(jnp.int32, (HB, BLK), 0) + l * HB
    at_column = lax.broadcasted_iota(jnp.int32, (HB, BLK), 1)
    spot = at_row == at_column
    columns = [jnp.zeros((1, BLK), jnp.float32) for _ in range(NB)]
    block_iota = lax.broadcasted_iota(jnp.int32, (NB, BLK), 0)
    held = []
    for p in range(N):
        code = jnp.concatenate([table[p : p + 1, :]] * (BLK // 128), axis=1)
        held.append((code > 0) & ((jnp.maximum(code - 1, 0) & 255) == block_iota))
    x_copies, rights = {}, []

    def arrived(j, *copies):
        if j == 0:

            @pl.when(r != 0)
            def _():
                for copy in copies:
                    copy.wait_recv()

        else:
            for copy in copies:
                copy.wait_recv()

    for j in range(J):
        arrived(j, c_copies[j])
        code = jnp.max(crecv[j])
        peer = jnp.maximum(code - 1, 0) // 256
        rights.append((code, peer))
        for dl in range(1, L):
            arrived(j, a_copies[j, dl])
            part = lax.dot_general(
                arow[j, part_rows(dl), :], feat[peer], CONTRACT_LAST, preferred_element_type=jnp.float32
            )
            xsend[j, dl - 1] = part.astype(jnp.bfloat16)
            copy = remote(
                xsend.at[j, dl - 1], xrecv.at[j, dl - 1], x_s.at[j, dl - 1], x_r.at[j, dl - 1], place(0, dl, 0)
            )
            copy.start()
            x_copies[j, dl] = copy

    for j in range(J):
        arrived(j, i_copies[j])
        inv_row = jnp.sum(jnp.where(spot, irecv[j], 0.0), axis=1, keepdims=True)
        inv_column = jnp.zeros((1, BLK), jnp.float32)
        for b in range(NB):
            inv_column = jnp.where(rights[j][1] == b, inv[b : b + 1, :], inv_column)
        scale[j] = 20.0 * (inv_row * inv_column)

    r_copies = []
    for j in range(J):
        arrived(j, a_copies[j, 0])
        dots = lax.dot_general(
            arow[j, part_rows(0), :], feat[rights[j][1]], CONTRACT_LAST, preferred_element_type=jnp.float32
        )
        for dl in range(1, L):
            x_copies[j, dl].wait_recv()
            dots = dots + xrecv[j, dl - 1].astype(jnp.float32)
        code, peer = rights[j]
        kern = jnp.exp(dots * scale[j])
        if j == 0:
            same = (r == 0) & ((jnp.maximum(code - 1, 0) & 255) == peer)
            kern = jnp.where(spot, kern * jnp.where(same, 0.0, 1.0), kern)
        row_sums = jnp.sum(kern, axis=1, keepdims=True)
        rsend[j] = jnp.sum(jnp.where(spot, row_sums, 0.0), axis=0, keepdims=True)
        column_sums = jnp.sum(kern, axis=0, keepdims=True)
        for b in range(NB):
            columns[b] = columns[b] + jnp.where((peer == b) & (code > 0), column_sums, 0.0)
        slot = e * L + l
        back = N - (R * j + r)
        for dl in range(L):
            for dr in range(R):
                k = dl * R + dr
                copy = remote(rsend.at[j], rrecv.at[slot], r_s.at[j, k], r_r.at[slot], place(back, dl, dr))
                if j == 0 and k == 0:

                    @pl.when(r == 0)
                    def _():
                        rrecv[slot] = rsend[0]

                    @pl.when(r != 0)
                    def _():
                        copy.start()

                else:
                    copy.start()
                r_copies.append(copy)

    mine_slot = l * R + r
    for b in range(NB):
        ctab[mine_slot, b : b + 1, :] = columns[b]
    t_copies = []
    for k in range(1, L * R):
        copy = remote(
            ctab.at[mine_slot], ctab.at[mine_slot], t_s.at[k - 1], t_r.at[k - 1], place(0, k // R, k % R)
        )
        copy.start()
        t_copies.append(copy)

    for k in range(1, L * R):
        t_copies[k - 1].wait()
    for d in range(N):
        p = lax.rem(e + d, N)
        for dl in range(L):
            slot = p * L + lax.rem(l + dl, L)
            copy = remote(rsend.at[0], rrecv.at[slot], r_s.at[0, 0], r_r.at[slot], place(0, 0, 1))
            if d == 0 and dl == 0:

                @pl.when(r != 0)
                def _():
                    copy.wait_recv()

            else:
                copy.wait_recv()

    totals = ctab[0]
    for i in range(1, L * R):
        totals = totals + ctab[i]
    for p in range(N):
        got = rrecv[p * L]
        for i in range(1, L):
            got = got + rrecv[p * L + i]
        totals = totals + jnp.where(held[p], got, 0.0)
    for b in range(NB):
        for h in range(BLK // 128):
            out[b * (BLK // 128) + h : b * (BLK // 128) + h + 1, :] = totals[b : b + 1, h * 128 : (h + 1) * 128]

    for copy in r_copies[1:] + list(x_copies.values()):
        copy.wait_send()
    for j in range(1, J):
        for copy in [c_copies[j], i_copies[j]] + [a_copies[j, dl] for dl in order]:
            copy.wait_send()

    @pl.when(r != 0)
    def _():
        for copy in [r_copies[0], c_copies[0], i_copies[0]] + [a_copies[0, dl] for dl in order]:
            copy.wait_send()


def on_device(sizes, features, pair_list, pair_count):
    N, L, R = sizes
    rows = features.shape[0]
    blocks = features.reshape(rows // BLK, BLK, -1)
    NB, _, width = blocks.shape
    J = N // R
    HB = BLK // L
    table_rows = -(-N // 8) * 8
    dma = pltpu.SemaphoreType.DMA
    vmem = pl.BlockSpec(memory_space=pltpu.VMEM)
    smem = pl.BlockSpec(memory_space=pltpu.SMEM)
    totals = pl.pallas_call(
        functools.partial(body, N, L, R),
        out_shape=jax.ShapeDtypeStruct((rows // 128, 128), jnp.float32),
        in_specs=[vmem, smem, smem],
        out_specs=vmem,
        scratch_shapes=[
            pltpu.VMEM((R, table_rows, 128), jnp.int32),
            pltpu.VMEM((J, BLK, width), jnp.bfloat16),
            pltpu.VMEM((J, BLK, width), jnp.bfloat16),
            pltpu.VMEM((J, 8, 128), jnp.int32),
            pltpu.VMEM((J, 8, 128), jnp.int32),
            pltpu.VMEM((L, NB, BLK), jnp.float32),
            pltpu.VMEM((J, 1, BLK), jnp.float32),
            pltpu.VMEM((J, 1, BLK), jnp.float32),
            pltpu.VMEM((J, L - 1, HB, BLK), jnp.bfloat16),
            pltpu.VMEM((J, L - 1, HB, BLK), jnp.bfloat16),
            pltpu.VMEM((J, 1, BLK), jnp.float32),
            pltpu.VMEM((N * L, 1, BLK), jnp.float32),
            pltpu.VMEM((L * R, NB, BLK), jnp.float32),
            pltpu.VMEM((J, HB, BLK), jnp.float32),
            dma((R - 1,)), dma((R - 1,)),
            dma((J, L)), dma((J, L)),
            dma((J,)), dma((J,)),
            dma((L - 1,)), dma((L - 1,)),
            dma((J,)), dma((J,)),
            dma((J, L - 1)), dma((J, L - 1)),
            dma((J, L * R)), dma((N * L,)),
            dma((L * R - 1,)), dma((L * R - 1,)),
        ],
        compiler_params=pltpu.CompilerParams(
            collective_id=0, has_side_effects=True, vmem_limit_bytes=48 * 1024 * 1024
        ),
    )(blocks, pair_list.transpose(1, 2, 0), pair_count)
    return jnp.log1p(totals / BLK).reshape(-1)


def solution(mesh):
    sizes = (mesh.shape["ex"], mesh.shape["layer"], mesh.shape["rep"])
    return jax.shard_map(
        functools.partial(on_device, sizes),
        mesh=mesh,
        in_specs=(
            P(("groups", "ex"), "layer", None),
            P(None, ("groups", "ex"), "rep"),
            P(("groups", "ex"), "rep"),
        ),
        out_specs=P(("groups", "ex")),
        check_vma=False,
    )
```
